32 devices in a mesh: groups: 2 (over y), wide: 4 (over z), narrow: 2 (over x), pair: 2 (over core).
Axes of the slice: x: 2, y: 2, z: 4, core: 2. Of those that a mesh axis runs over, the one named last changes fastest.
Arguments:
- psi: bfloat16 [4096, 2048], P(('groups', 'wide'), 'narrow'), parts along dimension 0, may hold values from -6 to 6
- left_ops: bfloat16 [128, 16, 128, 128], P(('groups', 'wide', 'pair')), parts along dimension 0, may hold values from -0.5 to 0.5
- right_ops: bfloat16 [128, 16, 128, 128], P(('groups', 'wide', 'pair'), 'narrow'), parts along dimension 0, may hold values from -0.0625 to 0.0625
- left_source: int32 [64, 16], P(('wide', 'pair')), may hold values from 0 to 15
- right_shift: int32 [64], P(('wide', 'pair')), may hold values from -1 to 1
- eps_left: float32 [4096], P(('groups', 'wide', 'pair')), parts along dimension 0, may hold values from -2 to 2
- eps_right: float32 [4096], P(('groups', 'narrow')), parts along dimension 0, may hold values from -2 to 2
Outputs:
- sigma: float32 [4096, 2048], P(('groups', 'wide', 'pair'), 'narrow'), parts along dimension 0
The draws below stay inside these ranges and needn't reach their ends.
There are 2 independent parts, one for each index of `groups`. The reference program is written for one: setup_inputs(seed, part) draws one part's arguments, and reference() takes and returns one part's arrays. A program takes and returns all parts, laid end to end along the dimension named above; an argument that names none is the same for every part. Nothing has to cross between parts.
All inputs are finite; a program needn't handle non-finite values.
Results may differ from the reference program's by a relative error of at most 0.0017.
Values may be sent and summed in bfloat16 or wider, within the bound.
A program may use at most 192 MiB of HBM per device.

```python
import jax
import jax.numpy as jnp
from jax import lax

BS = 128
M = 2048
NB = 16
TERMS = 64


def touch_ends(entries, rng, least, top_value):
    index_at = [jax.random.randint(jax.random.fold_in(rng, axis), (), 0, length) for axis, length in enumerate(entries.shape)]
    main_axis = entries.shape.index(max(entries.shape))
    neighbour = index_at[:main_axis] + [(index_at[main_axis] + 1) % entries.shape[main_axis]] + index_at[main_axis + 1:]
    return entries.at[tuple(index_at)].set(least).at[tuple(neighbour)].set(top_value)


def steps_of(stream_key, extent, split, low, high):
    loudness, own = 1.0, jax.random.fold_in(stream_key, 6)
    for dim, shards_of in split:
        heights = jnp.exp(jax.random.uniform(jax.random.fold_in(own, dim), (shards_of,), jnp.float32, low / len(split), high / len(split)))
        loudness = loudness * jnp.repeat(heights, extent[dim] // shards_of).reshape([-1 if axis == dim else 1 for axis in range(len(extent))])
    return loudness


def noise(own_key, dims, scale, bound, shards=(), kind=jnp.bfloat16):
    entries = jax.random.normal(own_key, dims, jnp.float32) * scale
    if len(shards) > 0:
        entries = steps_of(own_key, dims, shards, -0.22, 0.18) * entries
    return jnp.clip(entries, min=-bound, max=bound).astype(kind)


def setup_inputs(seed: int = 0, part: int = 0) -> dict:
    streams_of = jax.random.split(jax.random.key(seed), 8)
    own_keys = jax.random.split(jax.random.fold_in(streams_of[7], part), 8)
    psi = noise(own_keys[0], (M, M), 1.0, 6.0, ((0, 4), (1, 2)))
    left_ops = noise(own_keys[1], (TERMS, NB, BS, BS), BS ** -0.5, 0.5, ((0, 8),))
    right_ops = noise(own_keys[2], (TERMS, NB, BS, BS), (BS * TERMS) ** -0.5, 0.0625, ((0, 8), (1, 2)))
    left_source = touch_ends(jax.random.randint(streams_of[3], (TERMS, NB), 0, NB), jax.random.fold_in(streams_of[3], 1), 0, NB - 1).astype(jnp.int32)
    right_shift = touch_ends(jax.random.randint(streams_of[4], (TERMS,), -1, 2), jax.random.fold_in(streams_of[4], 1), -1, 1).astype(jnp.int32)
    eps_left = jnp.clip(jax.random.uniform(own_keys[5], (M,), jnp.float32, -2.0, 2.0) * steps_of(own_keys[5], (M,), ((0, 8),), -0.4, 0.0), -2.0, 2.0)
    eps_right = jnp.clip(jax.random.uniform(own_keys[6], (M,), jnp.float32, -2.0, 2.0) * steps_of(own_keys[6], (M,), ((0, 2),), -0.4, 0.0), -2.0, 2.0)
    return dict(psi=psi, left_ops=left_ops, right_ops=right_ops, left_source=left_source, right_shift=right_shift, eps_left=eps_left, eps_right=eps_right)


def reference(psi, left_ops, right_ops, left_source, right_shift, eps_left, eps_right):
    total = psi.shape[0]
    blocks = psi.reshape(NB, BS, total)

    def one_term(acc, items):
        left_t, right_t, source_t, shift_t = items
        picked = blocks[source_t]
        mixed = jnp.einsum("iab,ibw->iaw", left_t.astype(jnp.float32), picked.astype(jnp.float32)).astype(jnp.bfloat16)
        mixed = mixed.reshape(total, NB, BS)
        padded = jnp.pad(mixed, ((0, 0), (1, 1), (0, 0)))
        start = (1 - shift_t).astype(jnp.int32)
        shifted = lax.dynamic_slice(padded, (jnp.int32(0), start, jnp.int32(0)), (total, NB, BS))
        added = jnp.einsum("mjb,jab->mja", shifted.astype(jnp.float32), right_t.astype(jnp.float32))
        return acc + added.reshape(total, total), None

    hops, unused = lax.scan(one_term, jnp.zeros((total, total), jnp.float32), (left_ops, right_ops, left_source, right_shift))
    return hops + (eps_left[:, None] + eps_right[None, :]) * psi.astype(jnp.float32)
```

```python
import functools
import math

import jax
import jax.numpy as jnp
from jax import lax
from jax.experimental import pallas as pl
from jax.experimental.pallas import tpu as pltpu
from jax.sharding import PartitionSpec as P

MESH = pl.DeviceIdType.MESH
F32 = jnp.float32


def kernel(
    n, nx, block, wire,
    psi, left, right, meta_hbm, meta,
    out,
    panels, left_buf, right_buf, mixed, send_buf, recv_buf, meta_in, meta_other,
    psi_sem, own_sem, op_send, op_recv, z_send, z_recv, c_send, c_recv, h_send, h_recv,
    r_send, r_recv, m_sem,
):
    z, x, p = lax.axis_index("wide"), lax.axis_index("narrow"), lax.axis_index("pair")
    other = 1 - p
    terms = left.shape[0]
    blocks = right.shape[1]
    group = panels.shape[2]
    half, width = psi.shape[0] * group // 2, psi.shape[2]
    part_groups = half // group
    per_sector = block // group
    sectors = panels.shape[1] // per_sector

    own_panel = [
        pltpu.make_async_copy(
            psi.at[:, :, pl.ds(j * block, block)],
            panels.at[1 + j, pl.ds(z * 2 * part_groups, 2 * part_groups)],
            psi_sem.at[j],
        )
        for j in range(blocks)
    ]
    for copy in own_panel:
        copy.start()
    locals_ = [
        pltpu.make_async_copy(left.at[:, :, p], left_buf.at[pl.ds(0, terms)], own_sem.at[1]),
    ]
    for t in range(terms):
        locals_.append(
            pltpu.make_async_copy(
                right.at[t], right_buf.at[:, :, pl.ds(t * block, block)], own_sem.at[2 + t]
            )
        )
    for copy in locals_:
        copy.start()

    @pl.when(x == 0)
    def _():
        panels[0] = jnp.zeros(panels.shape[1:], panels.dtype)

    @pl.when(x == nx - 1)
    def _():
        panels[blocks + 1] = jnp.zeros(panels.shape[1:], panels.dtype)

    barrier = pltpu.get_barrier_semaphore()
    for k in range(1, n):
        pl.semaphore_signal(
            barrier, inc=1, device_id={"wide": lax.rem(z + k, n)}, device_id_type=MESH
        )
    pl.semaphore_signal(barrier, inc=1, device_id={"pair": other}, device_id_type=MESH)
    for sign in (-1, 1):
        @pl.when((x + sign >= 0) & (x + sign < nx))
        def _():
            for q in range(2):
                pl.semaphore_signal(
                    barrier, inc=1, device_id={"narrow": x + sign, "pair": q}, device_id_type=MESH
                )
    neighbours = jnp.where(x >= 1, 1, 0) + jnp.where(x < nx - 1, 1, 0)
    pl.semaphore_wait(barrier, n + 2 * neighbours)

    def rows_of(panel, part):
        return pl.ds((panel * 2 + part) * part_groups, part_groups)

    centre = pl.ds(1, blocks)

    def z_copy(stream, step):
        sign = 1 if stream == 0 else -1
        panel = z - sign * (step - 1)
        return pltpu.make_async_remote_copy(
            src_ref=panels.at[centre, rows_of(panel, p)],
            dst_ref=panels.at[centre, rows_of(panel, p)],
            send_sem=z_send.at[stream, step - 1],
            recv_sem=z_recv.at[stream, step - 1],
            device_id={"wide": z + sign},
            device_id_type=MESH,
        )

    def z_sends(stream, step):
        sign = 1 if stream == 0 else -1
        panel, to = z - sign * (step - 1), z + sign
        return (panel >= 0) & (panel < n) & (to >= 0) & (to < n)

    def z_gets(stream, step):
        sign = 1 if stream == 0 else -1
        panel = z - sign * step
        return (panel >= 0) & (panel < n)

    def z_arrival(stream, step):
        sign = 1 if stream == 0 else -1
        rows = rows_of(z - sign * step, p)
        return pltpu.make_async_remote_copy(
            src_ref=panels.at[centre, rows],
            dst_ref=panels.at[centre, rows],
            send_sem=z_send.at[stream, step - 1],
            recv_sem=z_recv.at[stream, step - 1],
            device_id={"wide": lax.rem(z + 1, n)},
            device_id_type=MESH,
        )

    def core_copy(stream, step):
        sign = 1 if stream == 0 else -1
        rows = rows_of(z - sign * step, p)
        return pltpu.make_async_remote_copy(
            src_ref=panels.at[centre, rows],
            dst_ref=panels.at[centre, rows],
            send_sem=c_send.at[stream, step - 1],
            recv_sem=c_recv.at[stream, step - 1],
            device_id={"pair": other},
            device_id_type=MESH,
        )

    def core_arrival(stream, step):
        sign = 1 if stream == 0 else -1
        rows = rows_of(z - sign * step, other)
        return pltpu.make_async_remote_copy(
            src_ref=panels.at[centre, rows],
            dst_ref=panels.at[centre, rows],
            send_sem=c_send.at[stream, step - 1],
            recv_sem=c_recv.at[stream, step - 1],
            device_id={"pair": other},
            device_id_type=MESH,
        )

    def edge_copy(slot, panel, way, q):
        sign = -1 if way == 0 else 1
        first = 1 if way == 0 else blocks
        into = blocks + 1 if way == 0 else 0
        return pltpu.make_async_remote_copy(
            src_ref=panels.at[first, rows_of(panel, p)],
            dst_ref=panels.at[into, rows_of(panel, p)],
            send_sem=h_send.at[way, slot, q],
            recv_sem=h_recv.at[way, slot, p],
            device_id={"narrow": x + sign, "pair": q},
            device_id_type=MESH,
        )

    def edge_arrival(slot, panel, way, q):
        into = blocks + 1 if way == 0 else 0
        ref = panels.at[into, rows_of(panel, q)]
        return pltpu.make_async_remote_copy(
            src_ref=ref,
            dst_ref=ref,
            send_sem=h_send.at[way, slot, q],
            recv_sem=h_recv.at[way, slot, q],
            device_id={"pair": other},
            device_id_type=MESH,
        )

    def edge_sends(way):
        return x >= 1 if way == 0 else x < nx - 1

    def edge_gets(way):
        return x < nx - 1 if way == 0 else x >= 1

    def start_edges(slot, panel):
        for way in range(2):
            @pl.when(edge_sends(way))
            def _():
                for q in range(2):
                    edge_copy(slot, panel, way, q).start()

    def panel_of(stream, step):
        return z - step if stream == 0 else z + step

    def slot_of(stream, step):
        return step if stream == 0 else n - 1 + step

    for copy in own_panel:
        copy.wait()
    for stream in range(2):
        @pl.when(z_sends(stream, 1))
        def _():
            z_copy(stream, 1).start()
    op_copies = [
        pltpu.make_async_remote_copy(
            src_ref=meta_hbm, dst_ref=meta_in, send_sem=op_send.at[0], recv_sem=op_recv.at[0],
            device_id={"pair": other}, device_id_type=MESH,
        ),
        pltpu.make_async_remote_copy(
            src_ref=left.at[:, :, other], dst_ref=left_buf.at[pl.ds(terms, terms)],
            send_sem=op_send.at[1], recv_sem=op_recv.at[1],
            device_id={"pair": other}, device_id_type=MESH,
        ),
    ]
    for t in range(terms):
        op_copies.append(
            pltpu.make_async_remote_copy(
                src_ref=right.at[t],
                dst_ref=right_buf.at[:, :, pl.ds((terms + t) * block, block)],
                send_sem=op_send.at[2 + t], recv_sem=op_recv.at[2 + t],
                device_id={"pair": other}, device_id_type=MESH,
            )
        )
    for copy in op_copies:
        copy.start()
    start_edges(0, z)

    for step in range(1, n):
        for stream in range(2):
            @pl.when(z_gets(stream, step))
            def _():
                z_arrival(stream, step).wait_recv()
                if step < n - 1:
                    @pl.when(z_sends(stream, step + 1))
                    def _():
                        z_copy(stream, step + 1).start()
                core_copy(stream, step).start()
                start_edges(slot_of(stream, step), panel_of(stream, step))

    for copy in locals_:
        copy.wait()
    for copy in op_copies:
        copy.wait_recv()
    fetch = pltpu.make_async_copy(meta_in, meta_other, m_sem)
    fetch.start()
    fetch.wait()
    for way in range(2):
        @pl.when(edge_gets(way))
        def _():
            for q in range(2):
                edge_arrival(0, z, way, q).wait_recv()
    for step in range(1, n):
        for stream in range(2):
            @pl.when(z_gets(stream, step))
            def _():
                core_arrival(stream, step).wait_recv()
                for way in range(2):
                    @pl.when(edge_gets(way))
                    def _():
                        for q in range(2):
                            edge_arrival(
                                slot_of(stream, step), panel_of(stream, step), way, q
                            ).wait_recv()

    def mix(dest):
        def one(t, source):
            first = 1 - source[t, sectors]
            slot = t if source is meta else t + terms
            for g in range(part_groups):
                sector = (dest * 2 * half + p * half + g * group) // block
                at = source[t, sector] * per_sector
                picked = jnp.concatenate(
                    [
                        jnp.concatenate([panels[first + j, at + u] for u in range(per_sector)], axis=0)
                        for j in range(blocks)
                    ],
                    axis=1,
                )
                value = jnp.dot(
                    left_buf[slot, dest, pl.ds(g * group, group), :], picked,
                    preferred_element_type=F32,
                ).astype(jnp.bfloat16)
                for j in range(blocks):
                    mixed[
                        j, pl.ds(g * group, group), pl.ds(pl.multiple_of(slot * block, block), block)
                    ] = value[:, j * block:(j + 1) * block]

        @pl.loop(0, terms)
        def _(t):
            one(t, meta)
            one(t, meta_other)

    def added(j):
        return lax.dot_general(
            mixed[j], right_buf[j], (((1,), (1,)), ((), ())), preferred_element_type=F32
        )

    def sum_copy(k):
        return pltpu.make_async_remote_copy(
            src_ref=send_buf.at[k - 1],
            dst_ref=recv_buf.at[k - 1],
            send_sem=r_send.at[k - 1],
            recv_sem=r_recv.at[k - 1],
            device_id={"wide": lax.rem(z + k, n)},
            device_id_type=MESH,
        )

    @pl.loop(0, n - 1)
    def _(m):
        k = 1 + lax.rem(n // 2 - 1 + m, n - 1)
        mix(lax.rem(z + k, n))
        for j in range(blocks):
            send_buf[k - 1, :, pl.ds(j * block, block)] = added(j).astype(wire)
        sum_copy(k).start()

    mix(z)
    for j in range(blocks):
        out[:, pl.ds(j * block, block)] = added(j)

    for stream in range(2):
        for step in range(1, n):
            @pl.when(z_sends(stream, step))
            def _():
                z_copy(stream, step).wait_send()

            @pl.when(z_gets(stream, step))
            def _():
                core_copy(stream, step).wait_send()
                for way in range(2):
                    @pl.when(edge_sends(way))
                    def _():
                        for q in range(2):
                            edge_copy(
                                slot_of(stream, step), panel_of(stream, step), way, q
                            ).wait_send()
    for way in range(2):
        @pl.when(edge_sends(way))
        def _():
            for q in range(2):
                edge_copy(0, z, way, q).wait_send()
    for copy in op_copies:
        copy.wait_send()

    @pl.loop(0, n - 1)
    def _(m):
        k = 1 + lax.rem(n // 2 - 1 + m, n - 1)
        sum_copy(k).wait_recv()
        out[...] += recv_buf[k - 1].astype(F32)
        sum_copy(k).wait_send()


def local(n, nx, psi, left_ops, right_ops, left_source, right_shift, eps_left, eps_right):
    block = left_ops.shape[2]
    owned_terms, sectors = left_ops.shape[:2]
    out_rows = eps_left.shape[0]
    width = psi.shape[1]
    blocks = right_ops.shape[1]
    total = sectors * block
    terms = 2 * owned_terms
    group = math.gcd(out_rows, block)
    wire = jnp.bfloat16
    left = left_ops.reshape(owned_terms, n, 2, out_rows, block)
    meta = jnp.concatenate([left_source, right_shift[:, None]], axis=1)
    meta = jnp.pad(meta, ((0, -owned_terms % 8), (0, -(sectors + 1) % 128)))
    slots = 2 * n - 1
    dma = pltpu.SemaphoreType.DMA
    hops = pl.pallas_call(
        functools.partial(kernel, n, nx, block, wire),
        out_shape=jax.ShapeDtypeStruct((out_rows, width), F32),
        in_specs=[pl.BlockSpec(memory_space=pl.ANY)] * 4
        + [pl.BlockSpec(memory_space=pltpu.SMEM)],
        out_specs=pl.BlockSpec(memory_space=pltpu.VMEM),
        scratch_shapes=[
            pltpu.VMEM((blocks + 2, total // group, group, block), jnp.bfloat16),
            pltpu.VMEM((terms, n, out_rows, block), jnp.bfloat16),
            pltpu.VMEM((blocks, block, terms * block), jnp.bfloat16),
            pltpu.VMEM((blocks, out_rows, terms * block), jnp.bfloat16),
            pltpu.VMEM((n - 1, out_rows, width), wire),
            pltpu.VMEM((n - 1, out_rows, width), wire),
            pltpu.VMEM(meta.shape, jnp.int32),
            pltpu.SMEM(meta.shape, jnp.int32),
            dma((blocks,)),
            dma((2 + owned_terms,)),
            dma((2 + owned_terms,)),
            dma((2 + owned_terms,)),
            dma((2, n - 1)),
            dma((2, n - 1)),
            dma((2, n - 1)),
            dma((2, n - 1)),
            dma((2, slots, 2)),
            dma((2, slots, 2)),
            dma((n - 1,)),
            dma((n - 1,)),
            dma(()),
        ],
        compiler_params=pltpu.CompilerParams(
            collective_id=0, has_side_effects=True, vmem_limit_bytes=48 * 1024 * 1024
        ),
        cost_estimate=pl.CostEstimate(
            flops=4 * terms * n * out_rows * block * width,
            bytes_accessed=2 * (psi.size + left_ops.size + right_ops.size),
            transcendentals=0,
        ),
    )(psi.reshape(-1, group, width), left, right_ops, meta, meta)
    own = lax.dynamic_slice_in_dim(psi, lax.axis_index("pair") * out_rows, out_rows, 0).astype(F32)
    return hops + (eps_left[:, None] + eps_right[None, :]) * own


def solution(mesh):
    in_specs = (
        P(("groups", "wide"), "narrow"),
        P(("groups", "wide", "pair"), None, None, None),
        P(("groups", "wide", "pair"), "narrow", None, None),
        P(("wide", "pair"), None),
        P(("wide", "pair")),
        P(("groups", "wide", "pair")),
        P(("groups", "narrow")),
    )
    out_specs = P(("groups", "wide", "pair"), "narrow")
    body = functools.partial(local, mesh.shape["wide"], mesh.shape["narrow"])
    return jax.shard_map(body, mesh=mesh, in_specs=in_specs, out_specs=out_specs, check_vma=False)
```

```python
import functools
import math

import jax
import jax.numpy as jnp
from jax import lax
from jax.experimental import pallas as pl
from jax.experimental.pallas import tpu as pltpu
from jax.sharding import PartitionSpec as P

MESH = pl.DeviceIdType.MESH
F32 = jnp.float32


def kernel(
    n, nx, block, chunks, wire,
    psi, left, right, meta_hbm, meta,
    out, *scratch,
):
    panels, scratch = scratch[:chunks], scratch[chunks:]
    (
        left_buf, right_buf, mixed, send_buf, recv_buf, meta_in, meta_other,
        psi_sem, own_sem, op_send, op_recv, z_send, z_recv, c_send, c_recv, h_send, h_recv,
        r_send, r_recv, m_sem, d_sem,
    ) = scratch
    z, x, p = lax.axis_index("wide"), lax.axis_index("narrow"), lax.axis_index("pair")
    other = 1 - p
    terms = left.shape[0]
    blocks = right.shape[1]
    per_chunk = blocks // chunks
    group = panels[0].shape[2]
    half = psi.shape[0] * group // 2
    part_groups = half // group
    per_sector = block // group
    sectors = panels[0].shape[1] // per_sector

    odd = lax.rem(x, 2)
    sign_x = 2 * odd - 1

    def column(o):
        return odd * o + (1 - odd) * (blocks - 1 - o)

    def span(c):
        first = 1 if c == 0 else 2
        last = per_chunk if c == chunks - 1 else per_chunk + 1
        return first, last

    own_panel = [[] for _ in range(chunks)]
    for c in range(chunks):
        for pos in range(span(c)[0], span(c)[1] + 1):
            o = c * per_chunk + pos - 1
            own_panel[c].append(
                pltpu.make_async_copy(
                    psi.at[:, :, pl.ds(pl.multiple_of(column(o) * block, block), block)],
                    panels[c].at[pos, pl.ds(z * 2 * part_groups, 2 * part_groups)],
                    psi_sem.at[o],
                )
            )
    for copies in own_panel:
        for copy in copies:
            copy.start()
    locals_ = [
        pltpu.make_async_copy(left.at[:, :, p], left_buf.at[pl.ds(0, terms)], own_sem.at[0]),
    ]
    for t in range(terms):
        locals_.append(
            pltpu.make_async_copy(
                right.at[t], right_buf.at[:, :, pl.ds(t * block, block)], own_sem.at[1 + t]
            )
        )
    for copy in locals_:
        copy.start()

    def beside(way):
        return x - sign_x if way == 0 else x + sign_x

    def has(way):
        return (beside(way) >= 0) & (beside(way) < nx)

    for way in range(2):
        @pl.when(jnp.logical_not(has(way)))
        def _():
            ref = panels[0] if way == 0 else panels[chunks - 1]
            ref[0 if way == 0 else per_chunk + 1] = jnp.zeros(ref.shape[1:], ref.dtype)

    barrier = pltpu.get_barrier_semaphore()
    for k in range(1, n):
        pl.semaphore_signal(
            barrier, inc=1, device_id={"wide": lax.rem(z + k, n)}, device_id_type=MESH
        )
    pl.semaphore_signal(barrier, inc=1, device_id={"pair": other}, device_id_type=MESH)
    for way in range(2):
        @pl.when(has(way))
        def _():
            for q in range(2):
                pl.semaphore_signal(
                    barrier, inc=1, device_id={"narrow": beside(way), "pair": q},
                    device_id_type=MESH,
                )
    neighbours = jnp.where(x >= 1, 1, 0) + jnp.where(x < nx - 1, 1, 0)
    pl.semaphore_wait(barrier, n + 2 * neighbours)

    def rows_of(panel, part):
        return pl.ds((panel * 2 + part) * part_groups, part_groups)

    def gathered(c, rows):
        first, last = span(c)
        return panels[c].at[pl.ds(first, last - first + 1), rows]

    def remote(src, dst, send, recv, device):
        return pltpu.make_async_remote_copy(
            src_ref=src, dst_ref=dst, send_sem=send, recv_sem=recv, device_id=device,
            device_id_type=MESH,
        )

    def panel_of(stream, step):
        return z - step if stream == 0 else z + step

    def z_copy(c, stream, step):
        ref = gathered(c, rows_of(panel_of(stream, step - 1), p))
        to = z + 1 if stream == 0 else z - 1
        return remote(
            ref, ref, z_send.at[c, stream, step - 1], z_recv.at[c, stream, step - 1], {"wide": to}
        )

    def z_sends(stream, step):
        panel, to = panel_of(stream, step - 1), z + 1 if stream == 0 else z - 1
        return (panel >= 0) & (panel < n) & (to >= 0) & (to < n)

    def z_gets(stream, step):
        panel = panel_of(stream, step)
        return (panel >= 0) & (panel < n)

    def z_arrival(c, stream, step):
        ref = gathered(c, rows_of(panel_of(stream, step), p))
        return remote(
            ref, ref, z_send.at[c, stream, step - 1], z_recv.at[c, stream, step - 1],
            {"wide": lax.rem(z + 1, n)},
        )

    def core_copy(c, stream, step, part):
        ref = gathered(c, rows_of(panel_of(stream, step), part))
        return remote(
            ref, ref, c_send.at[c, stream, step - 1], c_recv.at[c, stream, step - 1],
            {"pair": other},
        )

    def edge_refs(way, rows):
        if way == 0:
            return panels[0].at[1, rows], panels[0].at[0, rows]
        ref = panels[chunks - 1]
        return ref.at[per_chunk, rows], ref.at[per_chunk + 1, rows]

    def edge_copy(slot, panel, way, q):
        src, dst = edge_refs(way, rows_of(panel, p))
        return remote(
            src, dst, h_send.at[way, slot, q], h_recv.at[way, slot, p],
            {"narrow": beside(way), "pair": q},
        )

    def edge_arrival(slot, panel, way, q):
        ref = edge_refs(way, rows_of(panel, q))[1]
        return remote(ref, ref, h_send.at[way, slot, q], h_recv.at[way, slot, q], {"pair": other})

    def ways(c):
        return ([0] if c == 0 else []) + ([1] if c == chunks - 1 else [])

    def each_edge(c, slot, panel, act):
        for way in ways(c):
            @pl.when(has(way))
            def _():
                for q in range(2):
                    act(slot, panel, way, q)

    def slot_of(stream, step):
        return step if stream == 0 else n - 1 + step

    def gather_start(c):
        for copy in own_panel[c]:
            copy.wait()
        for stream in range(2):
            @pl.when(z_sends(stream, 1))
            def _():
                z_copy(c, stream, 1).start()
        each_edge(c, 0, z, lambda *a: edge_copy(*a).start())

    def gather_step(c, step):
        for stream in range(2):
            @pl.when(z_gets(stream, step))
            def _():
                z_arrival(c, stream, step).wait_recv()
                if step < n - 1:
                    @pl.when(z_sends(stream, step + 1))
                    def _():
                        z_copy(c, stream, step + 1).start()
                core_copy(c, stream, step, p).start()
                each_edge(
                    c, slot_of(stream, step), panel_of(stream, step),
                    lambda *a: edge_copy(*a).start(),
                )
        if step == n - 1 and c + 1 < chunks:
            gather_start(c + 1)

    def gather_finish(c):
        if c > 0:
            ties = [
                pltpu.make_async_copy(panels[c - 1].at[per_chunk + i], panels[c].at[i], d_sem.at[i])
                for i in range(2)
            ]
            for copy in ties:
                copy.start()
        each_edge(c, 0, z, lambda *a: edge_arrival(*a).wait_recv())
        for step in range(1, n):
            for stream in range(2):
                @pl.when(z_gets(stream, step))
                def _():
                    core_copy(c, stream, step, other).wait_recv()
                    each_edge(
                        c, slot_of(stream, step), panel_of(stream, step),
                        lambda *a: edge_arrival(*a).wait_recv(),
                    )
        if c > 0:
            for copy in ties:
                copy.wait()

    gather_start(0)
    op_copies = [
        remote(meta_hbm, meta_in, op_send.at[0], op_recv.at[0], {"pair": other}),
        remote(
            left.at[:, :, other], left_buf.at[pl.ds(terms, terms)], op_send.at[1], op_recv.at[1],
            {"pair": other},
        ),
    ]
    for t in range(terms):
        op_copies.append(
            remote(
                right.at[t], right_buf.at[:, :, pl.ds((terms + t) * block, block)],
                op_send.at[2 + t], op_recv.at[2 + t], {"pair": other},
            )
        )
    for copy in op_copies:
        copy.start()
    for step in range(1, n):
        gather_step(0, step)
    for copy in locals_:
        copy.wait()
    for copy in op_copies:
        copy.wait_recv()
    fetch = pltpu.make_async_copy(meta_in, meta_other, m_sem)
    fetch.start()
    fetch.wait()

    def mix(c, dest):
        def one(t, source):
            first = 1 - sign_x * source[t, sectors]
            slot = t if source is meta else t + terms
            for g in range(part_groups):
                sector = (dest * 2 * half + p * half + g * group) // block
                at = source[t, sector] * per_sector
                picked = jnp.concatenate(
                    [
                        jnp.concatenate(
                            [panels[c][first + j, at + u] for u in range(per_sector)], axis=0
                        )
                        for j in range(per_chunk)
                    ],
                    axis=1,
                )
                value = jnp.dot(
                    left_buf[slot, dest, pl.ds(g * group, group), :], picked,
                    preferred_element_type=F32,
                ).astype(jnp.bfloat16)
                for j in range(per_chunk):
                    mixed[
                        j, pl.ds(g * group, group), pl.ds(pl.multiple_of(slot * block, block), block)
                    ] = value[:, j * block:(j + 1) * block]

        @pl.loop(0, terms)
        def _(t):
            one(t, meta)
            one(t, meta_other)

    def added(c, j):
        return lax.dot_general(
            mixed[j], right_buf[column(c * per_chunk + j)], (((1,), (1,)), ((), ())),
            preferred_element_type=F32,
        )

    def sum_copy(c, k):
        return remote(
            send_buf.at[c, k - 1], recv_buf.at[c, k - 1], r_send.at[c, k - 1], r_recv.at[c, k - 1],
            {"wide": lax.rem(z + k, n)},
        )

    def turn(m):
        return 1 + lax.rem(n // 2 - 1 + m, n - 1)

    def place(o):
        return pl.ds(pl.multiple_of(column(o) * block, block), block)

    def part(c, m):
        k = turn(m)
        mix(c, lax.rem(z + k, n))
        for j in range(per_chunk):
            send_buf[c, k - 1, j] = added(c, j).astype(wire)
        sum_copy(c, k).start()

    for c in range(chunks):
        gather_finish(c)
        if c + 1 < chunks:
            for m in range(n - 1):
                part(c, jnp.int32(m))
                gather_step(c + 1, m + 1)
        else:
            pl.loop(0, n - 1)(functools.partial(part, c))
        mix(c, z)
        for j in range(per_chunk):
            out[:, place(c * per_chunk + j)] = added(c, j)

    for c in range(chunks):
        @pl.loop(0, n - 1)
        def _(m):
            k = turn(m)
            sum_copy(c, k).wait_recv()
            for j in range(per_chunk):
                out[:, place(c * per_chunk + j)] += recv_buf[c, k - 1, j].astype(F32)
            sum_copy(c, k).wait_send()

    for c in range(chunks):
        each_edge(c, 0, z, lambda *a: edge_copy(*a).wait_send())
        for stream in range(2):
            for step in range(1, n):
                @pl.when(z_sends(stream, step))
                def _():
                    z_copy(c, stream, step).wait_send()

                @pl.when(z_gets(stream, step))
                def _():
                    core_copy(c, stream, step, p).wait_send()
                    each_edge(
                        c, slot_of(stream, step), panel_of(stream, step),
                        lambda *a: edge_copy(*a).wait_send(),
                    )
    for copy in op_copies:
        copy.wait_send()


def local(n, nx, psi, left_ops, right_ops, left_source, right_shift, eps_left, eps_right):
    block = left_ops.shape[2]
    owned_terms, sectors = left_ops.shape[:2]
    out_rows = eps_left.shape[0]
    width = psi.shape[1]
    blocks = right_ops.shape[1]
    total = sectors * block
    terms = 2 * owned_terms
    group = math.gcd(out_rows, block)
    wire = jnp.bfloat16
    left = left_ops.reshape(owned_terms, n, 2, out_rows, block)
    meta = jnp.concatenate([left_source, right_shift[:, None]], axis=1)
    meta = jnp.pad(meta, ((0, -owned_terms % 8), (0, -(sectors + 1) % 128)))
    slots = 2 * n - 1
    chunks = 4 if blocks % 4 == 0 and blocks >= 8 else 1
    per_chunk = blocks // chunks
    dma = pltpu.SemaphoreType.DMA
    hops = pl.pallas_call(
        functools.partial(kernel, n, nx, block, chunks, wire),
        out_shape=jax.ShapeDtypeStruct((out_rows, width), F32),
        in_specs=[pl.BlockSpec(memory_space=pl.ANY)] * 4
        + [pl.BlockSpec(memory_space=pltpu.SMEM)],
        out_specs=pl.BlockSpec(memory_space=pltpu.VMEM),
        scratch_shapes=[
            *[
                pltpu.VMEM((per_chunk + 2, total // group, group, block), jnp.bfloat16)
                for _ in range(chunks)
            ],
            pltpu.VMEM((terms, n, out_rows, block), jnp.bfloat16),
            pltpu.VMEM((blocks, block, terms * block), jnp.bfloat16),
            pltpu.VMEM((per_chunk, out_rows, terms * block), jnp.bfloat16),
            pltpu.VMEM((chunks, n - 1, per_chunk, out_rows, block), wire),
            pltpu.VMEM((chunks, n - 1, per_chunk, out_rows, block), wire),
            pltpu.VMEM(meta.shape, jnp.int32),
            pltpu.SMEM(meta.shape, jnp.int32),
            dma((blocks,)),
            dma((1 + owned_terms,)),
            dma((2 + owned_terms,)),
            dma((2 + owned_terms,)),
            dma((chunks, 2, n - 1)),
            dma((chunks, 2, n - 1)),
            dma((chunks, 2, n - 1)),
            dma((chunks, 2, n - 1)),
            dma((2, slots, 2)),
            dma((2, slots, 2)),
            dma((chunks, n - 1)),
            dma((chunks, n - 1)),
            dma(()),
            dma((2,)),
        ],
        compiler_params=pltpu.CompilerParams(
            collective_id=0, has_side_effects=True, vmem_limit_bytes=48 * 1024 * 1024
        ),
        cost_estimate=pl.CostEstimate(
            flops=4 * terms * n * out_rows * block * width,
            bytes_accessed=2 * (psi.size + left_ops.size + right_ops.size),
            transcendentals=0,
        ),
    )(psi.reshape(-1, group, width), left, right_ops, meta, meta)
    own = lax.dynamic_slice_in_dim(psi, lax.axis_index("pair") * out_rows, out_rows, 0).astype(F32)
    return hops + (eps_left[:, None] + eps_right[None, :]) * own


def solution(mesh):
    in_specs = (
        P(("groups", "wide"), "narrow"),
        P(("groups", "wide", "pair"), None, None, None),
        P(("groups", "wide", "pair"), "narrow", None, None),
        P(("wide", "pair"), None),
        P(("wide", "pair")),
        P(("groups", "wide", "pair")),
        P(("groups", "narrow")),
    )
    out_specs = P(("groups", "wide", "pair"), "narrow")
    body = functools.partial(local, mesh.shape["wide"], mesh.shape["narrow"])
    return jax.shard_map(body, mesh=mesh, in_specs=in_specs, out_specs=out_specs, check_vma=False)
```

```python
import functools
import math

import jax
import jax.numpy as jnp
from jax import lax
from jax.experimental import pallas as pl
from jax.experimental.pallas import tpu as pltpu
from jax.sharding import PartitionSpec as P

MESH = pl.DeviceIdType.MESH
F32 = jnp.float32


def kernel(
    n, nx, block, chunks, wire,
    psi, left, right, meta_hbm, meta,
    out, *scratch,
):
    panels, scratch = scratch[:chunks], scratch[chunks:]
    (
        left_buf, right_buf, mixed, send_buf, recv_buf, relay_buf, meta_in, meta_other,
        psi_sem, own_sem, op_send, op_recv, z_send, z_recv, c_send, c_recv, h_send, h_recv,
        r_send, r_recv, l_send, l_recv, m_sem, d_sem,
    ) = scratch
    z, x, p = lax.axis_index("wide"), lax.axis_index("narrow"), lax.axis_index("pair")
    other = 1 - p
    terms = left.shape[0]
    blocks = right.shape[1]
    per_chunk = blocks // chunks
    group = panels[0].shape[2]
    half = psi.shape[0] * group // 2
    part_groups = half // group
    per_sector = block // group
    sectors = panels[0].shape[1] // per_sector

    odd = lax.rem(x, 2)
    sign_x = 2 * odd - 1

    def column(o):
        return odd * o + (1 - odd) * (blocks - 1 - o)

    def span(c):
        first = 1 if c == 0 else 2
        last = per_chunk if c == chunks - 1 else per_chunk + 1
        return first, last

    own_panel = [[] for _ in range(chunks)]
    for c in range(chunks):
        for pos in range(span(c)[0], span(c)[1] + 1):
            o = c * per_chunk + pos - 1
            own_panel[c].append(
                pltpu.make_async_copy(
                    psi.at[:, :, pl.ds(pl.multiple_of(column(o) * block, block), block)],
                    panels[c].at[pos, pl.ds(z * 2 * part_groups, 2 * part_groups)],
                    psi_sem.at[o],
                )
            )
    for copies in own_panel:
        for copy in copies:
            copy.start()
    locals_ = [
        pltpu.make_async_copy(left.at[:, :, p], left_buf.at[pl.ds(0, terms)], own_sem.at[0]),
    ]
    for t in range(terms):
        locals_.append(
            pltpu.make_async_copy(
                right.at[t], right_buf.at[:, :, pl.ds(t * block, block)], own_sem.at[1 + t]
            )
        )
    for copy in locals_:
        copy.start()

    def beside(way):
        return x - sign_x if way == 0 else x + sign_x

    def has(way):
        return (beside(way) >= 0) & (beside(way) < nx)

    for way in range(2):
        @pl.when(jnp.logical_not(has(way)))
        def _():
            ref = panels[0] if way == 0 else panels[chunks - 1]
            ref[0 if way == 0 else per_chunk + 1] = jnp.zeros(ref.shape[1:], ref.dtype)

    barrier = pltpu.get_barrier_semaphore()
    for k in range(1, n):
        pl.semaphore_signal(
            barrier, inc=1, device_id={"wide": lax.rem(z + k, n)}, device_id_type=MESH
        )
    pl.semaphore_signal(barrier, inc=1, device_id={"pair": other}, device_id_type=MESH)
    for way in range(2):
        @pl.when(has(way))
        def _():
            for q in range(2):
                pl.semaphore_signal(
                    barrier, inc=1, device_id={"narrow": beside(way), "pair": q},
                    device_id_type=MESH,
                )
    neighbours = jnp.where(x >= 1, 1, 0) + jnp.where(x < nx - 1, 1, 0)
    pl.semaphore_wait(barrier, n + 2 * neighbours)

    def rows_of(panel, part):
        return pl.ds((panel * 2 + part) * part_groups, part_groups)

    def gathered(c, rows):
        first, last = span(c)
        return panels[c].at[pl.ds(first, last - first + 1), rows]

    def remote(src, dst, send, recv, device):
        return pltpu.make_async_remote_copy(
            src_ref=src, dst_ref=dst, send_sem=send, recv_sem=recv, device_id=device,
            device_id_type=MESH,
        )

    def panel_of(stream, step):
        return z - step if stream == 0 else z + step

    def z_copy(c, stream, step):
        ref = gathered(c, rows_of(panel_of(stream, step - 1), p))
        to = z + 1 if stream == 0 else z - 1
        return remote(
            ref, ref, z_send.at[c, stream, step - 1], z_recv.at[c, stream, step - 1], {"wide": to}
        )

    def z_sends(stream, step):
        panel, to = panel_of(stream, step - 1), z + 1 if stream == 0 else z - 1
        return (panel >= 0) & (panel < n) & (to >= 0) & (to < n)

    def z_gets(stream, step):
        panel = panel_of(stream, step)
        return (panel >= 0) & (panel < n)

    def z_arrival(c, stream, step):
        ref = gathered(c, rows_of(panel_of(stream, step), p))
        return remote(
            ref, ref, z_send.at[c, stream, step - 1], z_recv.at[c, stream, step - 1],
            {"wide": lax.rem(z + 1, n)},
        )

    def core_copy(c, stream, step, part):
        ref = gathered(c, rows_of(panel_of(stream, step), part))
        return remote(
            ref, ref, c_send.at[c, stream, step - 1], c_recv.at[c, stream, step - 1],
            {"pair": other},
        )

    def edge_refs(way, rows):
        if way == 0:
            return panels[0].at[1, rows], panels[0].at[0, rows]
        ref = panels[chunks - 1]
        return ref.at[per_chunk, rows], ref.at[per_chunk + 1, rows]

    def edge_copy(slot, panel, way, q):
        src, dst = edge_refs(way, rows_of(panel, p))
        return remote(
            src, dst, h_send.at[way, slot, q], h_recv.at[way, slot, p],
            {"narrow": beside(way), "pair": q},
        )

    def edge_arrival(slot, panel, way, q):
        ref = edge_refs(way, rows_of(panel, q))[1]
        return remote(ref, ref, h_send.at[way, slot, q], h_recv.at[way, slot, q], {"pair": other})

    def ways(c):
        return ([0] if c == 0 else []) + ([1] if c == chunks - 1 else [])

    def each_edge(c, slot, panel, act):
        for way in ways(c):
            @pl.when(has(way))
            def _():
                for q in range(2):
                    act(slot, panel, way, q)

    def slot_of(stream, step):
        return step if stream == 0 else n - 1 + step

    def gather_start(c):
        for copy in own_panel[c]:
            copy.wait()
        for stream in range(2):
            @pl.when(z_sends(stream, 1))
            def _():
                z_copy(c, stream, 1).start()
        each_edge(c, 0, z, lambda *a: edge_copy(*a).start())

    def gather_step(c, step):
        for stream in range(2):
            @pl.when(z_gets(stream, step))
            def _():
                z_arrival(c, stream, step).wait_recv()
                if step < n - 1:
                    @pl.when(z_sends(stream, step + 1))
                    def _():
                        z_copy(c, stream, step + 1).start()
                core_copy(c, stream, step, p).start()
                each_edge(
                    c, slot_of(stream, step), panel_of(stream, step),
                    lambda *a: edge_copy(*a).start(),
                )

    def gather_finish(c):
        if c > 0:
            ties = [
                pltpu.make_async_copy(panels[c - 1].at[per_chunk + i], panels[c].at[i], d_sem.at[i])
                for i in range(2)
            ]
            for copy in ties:
                copy.start()
        each_edge(c, 0, z, lambda *a: edge_arrival(*a).wait_recv())
        for step in range(1, n):
            for stream in range(2):
                @pl.when(z_gets(stream, step))
                def _():
                    core_copy(c, stream, step, other).wait_recv()
                    each_edge(
                        c, slot_of(stream, step), panel_of(stream, step),
                        lambda *a: edge_arrival(*a).wait_recv(),
                    )
        if c > 0:
            for copy in ties:
                copy.wait()

    for c in range(chunks):
        gather_start(c)
    op_copies = [
        remote(meta_hbm, meta_in, op_send.at[0], op_recv.at[0], {"pair": other}),
        remote(
            left.at[:, :, other], left_buf.at[pl.ds(terms, terms)], op_send.at[1], op_recv.at[1],
            {"pair": other},
        ),
    ]
    for t in range(terms):
        op_copies.append(
            remote(
                right.at[t], right_buf.at[:, :, pl.ds((terms + t) * block, block)],
                op_send.at[2 + t], op_recv.at[2 + t], {"pair": other},
            )
        )
    for copy in op_copies:
        copy.start()
    for step in range(1, n):
        gather_step(0, step)
    for copy in locals_:
        copy.wait()
    for copy in op_copies:
        copy.wait_recv()
    fetch = pltpu.make_async_copy(meta_in, meta_other, m_sem)
    fetch.start()
    fetch.wait()

    def mix(c, dest):
        def one(t, source):
            first = 1 - sign_x * source[t, sectors]
            slot = t if source is meta else t + terms
            for g in range(part_groups):
                sector = (dest * 2 * half + p * half + g * group) // block
                at = source[t, sector] * per_sector
                picked = jnp.concatenate(
                    [
                        jnp.concatenate(
                            [panels[c][first + j, at + u] for u in range(per_sector)], axis=0
                        )
                        for j in range(per_chunk)
                    ],
                    axis=1,
                )
                value = jnp.dot(
                    left_buf[slot, dest, pl.ds(g * group, group), :], picked,
                    preferred_element_type=F32,
                ).astype(jnp.bfloat16)
                for j in range(per_chunk):
                    mixed[
                        j, pl.ds(g * group, group), pl.ds(pl.multiple_of(slot * block, block), block)
                    ] = value[:, j * block:(j + 1) * block]

        @pl.loop(0, terms)
        def _(t):
            one(t, meta)
            one(t, meta_other)

    def added(c, j):
        return lax.dot_general(
            mixed[j], right_buf[column(c * per_chunk + j)], (((1,), (1,)), ((), ())),
            preferred_element_type=F32,
        )

    def sum_copy(c, k):
        return remote(
            send_buf.at[c, k - 1], recv_buf.at[c, k - 1], r_send.at[c, k - 1], r_recv.at[c, k - 1],
            {"wide": lax.rem(z + k, n)},
        )

    relay = n == 4
    low = jnp.where(z < 2, 1, -1)
    end = (z == 0) | (z == n - 1)
    far = 2 + low

    def turn(m):
        if not relay:
            return 1 + lax.rem(n // 2 - 1 + m, n - 1)
        middle = 2 + (low if m == 1 else -low if m == 0 else 0)
        return jnp.where(end, 2 + low * (1 - m), middle)

    def relay_copy(c):
        return remote(
            send_buf.at[c, far - 1], relay_buf.at[c], l_send.at[c], l_recv.at[c],
            {"wide": z + low},
        )

    def relay_arrival(c):
        return remote(
            relay_buf.at[c], relay_buf.at[c], l_send.at[c], l_recv.at[c], {"wide": z - low}
        )

    def place(o):
        return pl.ds(pl.multiple_of(column(o) * block, block), block)

    def part(c, m):
        k = turn(m)
        mix(c, lax.rem(z + k, n))
        if relay and m == n - 2:
            @pl.when(jnp.logical_not(end))
            def _():
                relay_arrival(c).wait_recv()
                for j in range(per_chunk):
                    send_buf[c, k - 1, j] = (added(c, j) + relay_buf[c, j].astype(F32)).astype(wire)

            @pl.when(end)
            def _():
                for j in range(per_chunk):
                    send_buf[c, k - 1, j] = added(c, j).astype(wire)
        else:
            for j in range(per_chunk):
                send_buf[c, k - 1, j] = added(c, j).astype(wire)
        if relay and m == 0:
            @pl.when(end)
            def _():
                relay_copy(c).start()

            @pl.when(jnp.logical_not(end))
            def _():
                sum_copy(c, k).start()
        else:
            sum_copy(c, k).start()

    for c in range(chunks):
        gather_finish(c)
        if c + 1 < chunks:
            for m in range(n - 1):
                part(c, m)
                gather_step(c + 1, m + 1)
        elif relay:
            for m in range(n - 1):
                part(c, m)
        else:
            pl.loop(0, n - 1)(functools.partial(part, c))
        mix(c, z)
        for j in range(per_chunk):
            out[:, place(c * per_chunk + j)] = added(c, j)

    def add_in(c, k):
        sum_copy(c, k).wait_recv()
        for j in range(per_chunk):
            out[:, place(c * per_chunk + j)] += recv_buf[c, k - 1, j].astype(F32)

    for c in range(chunks):
        if relay:
            for k in (2 - low, 2 + low):
                @pl.when((k == 2 + low) | jnp.logical_not(end))
                def _():
                    add_in(c, k)
            add_in(c, jnp.int32(2))
            for k in (2 - low, jnp.int32(2)):
                sum_copy(c, k).wait_send()

            @pl.when(end)
            def _():
                relay_copy(c).wait_send()

            @pl.when(jnp.logical_not(end))
            def _():
                sum_copy(c, far).wait_send()
        else:
            @pl.loop(0, n - 1)
            def _(m):
                k = turn(m)
                add_in(c, k)
                sum_copy(c, k).wait_send()

    for c in range(chunks):
        each_edge(c, 0, z, lambda *a: edge_copy(*a).wait_send())
        for stream in range(2):
            for step in range(1, n):
                @pl.when(z_sends(stream, step))
                def _():
                    z_copy(c, stream, step).wait_send()

                @pl.when(z_gets(stream, step))
                def _():
                    core_copy(c, stream, step, p).wait_send()
                    each_edge(
                        c, slot_of(stream, step), panel_of(stream, step),
                        lambda *a: edge_copy(*a).wait_send(),
                    )
    for copy in op_copies:
        copy.wait_send()


def local(n, nx, psi, left_ops, right_ops, left_source, right_shift, eps_left, eps_right):
    block = left_ops.shape[2]
    owned_terms, sectors = left_ops.shape[:2]
    out_rows = eps_left.shape[0]
    width = psi.shape[1]
    blocks = right_ops.shape[1]
    total = sectors * block
    terms = 2 * owned_terms
    group = math.gcd(out_rows, block)
    wire = jnp.bfloat16
    left = left_ops.reshape(owned_terms, n, 2, out_rows, block)
    meta = jnp.concatenate([left_source, right_shift[:, None]], axis=1)
    meta = jnp.pad(meta, ((0, -owned_terms % 8), (0, -(sectors + 1) % 128)))
    slots = 2 * n - 1
    chunks = 2 if blocks % 2 == 0 and blocks >= 4 else 1
    per_chunk = blocks // chunks
    dma = pltpu.SemaphoreType.DMA
    hops = pl.pallas_call(
        functools.partial(kernel, n, nx, block, chunks, wire),
        out_shape=jax.ShapeDtypeStruct((out_rows, width), F32),
        in_specs=[pl.BlockSpec(memory_space=pl.ANY)] * 4
        + [pl.BlockSpec(memory_space=pltpu.SMEM)],
        out_specs=pl.BlockSpec(memory_space=pltpu.VMEM),
        scratch_shapes=[
            *[
                pltpu.VMEM((per_chunk + 2, total // group, group, block), jnp.bfloat16)
                for _ in range(chunks)
            ],
            pltpu.VMEM((terms, n, out_rows, block), jnp.bfloat16),
            pltpu.VMEM((blocks, block, terms * block), jnp.bfloat16),
            pltpu.VMEM((per_chunk, out_rows, terms * block), jnp.bfloat16),
            pltpu.VMEM((chunks, n - 1, per_chunk, out_rows, block), wire),
            pltpu.VMEM((chunks, n - 1, per_chunk, out_rows, block), wire),
            pltpu.VMEM((chunks, per_chunk, out_rows, block), wire),
            pltpu.VMEM(meta.shape, jnp.int32),
            pltpu.SMEM(meta.shape, jnp.int32),
            dma((blocks,)),
            dma((1 + owned_terms,)),
            dma((2 + owned_terms,)),
            dma((2 + owned_terms,)),
            dma((chunks, 2, n - 1)),
            dma((chunks, 2, n - 1)),
            dma((chunks, 2, n - 1)),
            dma((chunks, 2, n - 1)),
            dma((2, slots, 2)),
            dma((2, slots, 2)),
            dma((chunks, n - 1)),
            dma((chunks, n - 1)),
            dma((chunks,)),
            dma((chunks,)),
            dma(()),
            dma((2,)),
        ],
        compiler_params=pltpu.CompilerParams(
            collective_id=0, has_side_effects=True, vmem_limit_bytes=48 * 1024 * 1024
        ),
        cost_estimate=pl.CostEstimate(
            flops=4 * terms * n * out_rows * block * width,
            bytes_accessed=2 * (psi.size + left_ops.size + right_ops.size),
            transcendentals=0,
        ),
    )(psi.reshape(-1, group, width), left, right_ops, meta, meta)
    own = lax.dynamic_slice_in_dim(psi, lax.axis_index("pair") * out_rows, out_rows, 0).astype(F32)
    return hops + (eps_left[:, None] + eps_right[None, :]) * own


def solution(mesh):
    in_specs = (
        P(("groups", "wide"), "narrow"),
        P(("groups", "wide", "pair"), None, None, None),
        P(("groups", "wide", "pair"), "narrow", None, None),
        P(("wide", "pair"), None),
        P(("wide", "pair")),
        P(("groups", "wide", "pair")),
        P(("groups", "narrow")),
    )
    out_specs = P(("groups", "wide", "pair"), "narrow")
    body = functools.partial(local, mesh.shape["wide"], mesh.shape["narrow"])
    return jax.shard_map(body, mesh=mesh, in_specs=in_specs, out_specs=out_specs, check_vma=False)
```

```python
import functools
import math

import jax
import jax.numpy as jnp
from jax import lax
from jax.experimental import pallas as pl
from jax.experimental.pallas import tpu as pltpu
from jax.sharding import PartitionSpec as P

MESH = pl.DeviceIdType.MESH
F32 = jnp.float32


def kernel(
    n, nx, block, chunks, wire,
    psi, left, right, meta_hbm, shift_hbm, meta, shift,
    out, *scratch,
):
    panels, scratch = scratch[:chunks], scratch[chunks:]
    (
        left_buf, right_buf, mixed, send_buf, recv_buf, relay_buf, meta_in, meta_other, shift_in, shift_other,
        psi_sem, own_sem, op_send, op_recv, z_send, z_recv, c_send, c_recv, h_send, h_recv,
        r_send, r_recv, l_send, l_recv, m_sem, d_sem,
    ) = scratch
    z, x, p = lax.axis_index("wide"), lax.axis_index("narrow"), lax.axis_index("pair")
    other = 1 - p
    terms = left.shape[0]
    blocks = right.shape[1]
    per_chunk = blocks // chunks
    group = panels[0].shape[2]
    half = psi.shape[0] * group // 2
    part_groups = half // group
    per_sector = block // group

    odd = lax.rem(x, 2)
    sign_x = 2 * odd - 1

    def column(o):
        return odd * o + (1 - odd) * (blocks - 1 - o)

    def span(c):
        first = 1 if c == 0 else 2
        last = per_chunk if c == chunks - 1 else per_chunk + 1
        return first, last

    own_panel = [[] for _ in range(chunks)]
    for c in range(chunks):
        for pos in range(span(c)[0], span(c)[1] + 1):
            o = c * per_chunk + pos - 1
            own_panel[c].append(
                pltpu.make_async_copy(
                    psi.at[:, :, pl.ds(pl.multiple_of(column(o) * block, block), block)],
                    panels[c].at[pos, pl.ds(z * 2 * part_groups, 2 * part_groups)],
                    psi_sem.at[o],
                )
            )
    for copies in own_panel:
        for copy in copies:
            copy.start()
    locals_ = [
        pltpu.make_async_copy(left.at[:, :, p], left_buf.at[pl.ds(0, terms)], own_sem.at[0]),
    ]
    for t in range(terms):
        locals_.append(
            pltpu.make_async_copy(
                right.at[t], right_buf.at[:, :, pl.ds(t * block, block)], own_sem.at[1 + t]
            )
        )
    for copy in locals_:
        copy.start()

    def beside(way):
        return x - sign_x if way == 0 else x + sign_x

    def has(way):
        return (beside(way) >= 0) & (beside(way) < nx)

    for way in range(2):
        @pl.when(jnp.logical_not(has(way)))
        def _():
            ref = panels[0] if way == 0 else panels[chunks - 1]
            ref[0 if way == 0 else per_chunk + 1] = jnp.zeros(ref.shape[1:], ref.dtype)

    barrier = pltpu.get_barrier_semaphore()
    for k in range(1, n):
        pl.semaphore_signal(
            barrier, inc=1, device_id={"wide": lax.rem(z + k, n)}, device_id_type=MESH
        )
    pl.semaphore_signal(barrier, inc=1, device_id={"pair": other}, device_id_type=MESH)
    for way in range(2):
        @pl.when(has(way))
        def _():
            for q in range(2):
                pl.semaphore_signal(
                    barrier, inc=1, device_id={"narrow": beside(way), "pair": q},
                    device_id_type=MESH,
                )
    neighbours = jnp.where(x >= 1, 1, 0) + jnp.where(x < nx - 1, 1, 0)
    pl.semaphore_wait(barrier, n + 2 * neighbours)

    def rows_of(panel, part):
        return pl.ds((panel * 2 + part) * part_groups, part_groups)

    def gathered(c, rows):
        first, last = span(c)
        return panels[c].at[pl.ds(first, last - first + 1), rows]

    def remote(src, dst, send, recv, device):
        return pltpu.make_async_remote_copy(
            src_ref=src, dst_ref=dst, send_sem=send, recv_sem=recv, device_id=device,
            device_id_type=MESH,
        )

    def panel_of(stream, step):
        return z - step if stream == 0 else z + step

    def z_copy(c, stream, step):
        ref = gathered(c, rows_of(panel_of(stream, step - 1), p))
        to = z + 1 if stream == 0 else z - 1
        return remote(
            ref, ref, z_send.at[c, stream, step - 1], z_recv.at[c, stream, step - 1], {"wide": to}
        )

    def z_sends(stream, step):
        panel, to = panel_of(stream, step - 1), z + 1 if stream == 0 else z - 1
        return (panel >= 0) & (panel < n) & (to >= 0) & (to < n)

    def z_gets(stream, step):
        panel = panel_of(stream, step)
        return (panel >= 0) & (panel < n)

    def z_arrival(c, stream, step):
        ref = gathered(c, rows_of(panel_of(stream, step), p))
        return remote(
            ref, ref, z_send.at[c, stream, step - 1], z_recv.at[c, stream, step - 1],
            {"wide": lax.rem(z + 1, n)},
        )

    def core_copy(c, stream, step, part):
        ref = gathered(c, rows_of(panel_of(stream, step), part))
        return remote(
            ref, ref, c_send.at[c, stream, step - 1], c_recv.at[c, stream, step - 1],
            {"pair": other},
        )

    def edge_refs(way, rows):
        if way == 0:
            return panels[0].at[1, rows], panels[0].at[0, rows]
        ref = panels[chunks - 1]
        return ref.at[per_chunk, rows], ref.at[per_chunk + 1, rows]

    def edge_copy(slot, panel, way, q):
        src, dst = edge_refs(way, rows_of(panel, p))
        return remote(
            src, dst, h_send.at[way, slot, q], h_recv.at[way, slot, p],
            {"narrow": beside(way), "pair": q},
        )

    def edge_arrival(slot, panel, way, q):
        ref = edge_refs(way, rows_of(panel, q))[1]
        return remote(ref, ref, h_send.at[way, slot, q], h_recv.at[way, slot, q], {"pair": other})

    def ways(c):
        return ([0] if c == 0 else []) + ([1] if c == chunks - 1 else [])

    def each_edge(c, slot, panel, act):
        for way in ways(c):
            @pl.when(has(way))
            def _():
                for q in range(2):
                    act(slot, panel, way, q)

    def slot_of(stream, step):
        return step if stream == 0 else n - 1 + step

    def gather_start(c):
        for copy in own_panel[c]:
            copy.wait()
        for stream in range(2):
            @pl.when(z_sends(stream, 1))
            def _():
                z_copy(c, stream, 1).start()
        each_edge(c, 0, z, lambda *a: edge_copy(*a).start())

    def gather_step(c, step):
        for stream in range(2):
            @pl.when(z_gets(stream, step))
            def _():
                z_arrival(c, stream, step).wait_recv()
                if step < n - 1:
                    @pl.when(z_sends(stream, step + 1))
                    def _():
                        z_copy(c, stream, step + 1).start()
                core_copy(c, stream, step, p).start()
                each_edge(
                    c, slot_of(stream, step), panel_of(stream, step),
                    lambda *a: edge_copy(*a).start(),
                )

    def gather_finish(c):
        if c > 0:
            ties = [
                pltpu.make_async_copy(panels[c - 1].at[per_chunk + i], panels[c].at[i], d_sem.at[i])
                for i in range(2)
            ]
            for copy in ties:
                copy.start()
        each_edge(c, 0, z, lambda *a: edge_arrival(*a).wait_recv())
        for step in range(1, n):
            for stream in range(2):
                @pl.when(z_gets(stream, step))
                def _():
                    core_copy(c, stream, step, other).wait_recv()
                    each_edge(
                        c, slot_of(stream, step), panel_of(stream, step),
                        lambda *a: edge_arrival(*a).wait_recv(),
                    )
        if c > 0:
            for copy in ties:
                copy.wait()

    for c in range(chunks):
        gather_start(c)
    op_copies = [
        remote(meta_hbm, meta_in, op_send.at[0], op_recv.at[0], {"pair": other}),
        remote(
            shift_hbm, shift_in, op_send.at[2 + terms], op_recv.at[2 + terms], {"pair": other}
        ),
        remote(
            left.at[:, :, other], left_buf.at[pl.ds(terms, terms)], op_send.at[1], op_recv.at[1],
            {"pair": other},
        ),
    ]
    for t in range(terms):
        op_copies.append(
            remote(
                right.at[t], right_buf.at[:, :, pl.ds((terms + t) * block, block)],
                op_send.at[2 + t], op_recv.at[2 + t], {"pair": other},
            )
        )
    for copy in op_copies:
        copy.start()
    for step in range(1, n):
        gather_step(0, step)
    for copy in locals_:
        copy.wait()
    for copy in op_copies:
        copy.wait_recv()
    fetches = [
        pltpu.make_async_copy(meta_in, meta_other, m_sem.at[0]),
        pltpu.make_async_copy(shift_in, shift_other, m_sem.at[1]),
    ]
    for copy in fetches:
        copy.start()
    for copy in fetches:
        copy.wait()

    def mix(c, dest):
        def one(t, source, moved):
            first = 1 - sign_x * moved[0, t]
            slot = t if source is meta else t + terms
            for g in range(part_groups):
                sector = (dest * 2 * half + p * half + g * group) // block
                at = source[t, sector] * per_sector
                picked = jnp.concatenate(
                    [
                        jnp.concatenate(
                            [panels[c][first + j, at + u] for u in range(per_sector)], axis=0
                        )
                        for j in range(per_chunk)
                    ],
                    axis=1,
                )
                value = jnp.dot(
                    left_buf[slot, dest, pl.ds(g * group, group), :], picked,
                    preferred_element_type=F32,
                ).astype(jnp.bfloat16)
                for j in range(per_chunk):
                    mixed[
                        j, pl.ds(g * group, group), pl.ds(pl.multiple_of(slot * block, block), block)
                    ] = value[:, j * block:(j + 1) * block]

        @pl.loop(0, terms)
        def _(t):
            one(t, meta, shift)
            one(t, meta_other, shift_other)

    def added(c, j):
        return lax.dot_general(
            mixed[j], right_buf[column(c * per_chunk + j)], (((1,), (1,)), ((), ())),
            preferred_element_type=F32,
        )

    def sum_copy(c, k):
        return remote(
            send_buf.at[c, k - 1], recv_buf.at[c, k - 1], r_send.at[c, k - 1], r_recv.at[c, k - 1],
            {"wide": lax.rem(z + k, n)},
        )

    relay = n == 4
    low = jnp.where(z < 2, 1, -1)
    end = (z == 0) | (z == n - 1)
    far = 2 + low

    def turn(m):
        if not relay:
            return 1 + lax.rem(n // 2 - 1 + m, n - 1)
        middle = 2 + (low if m == 1 else -low if m == 0 else 0)
        return jnp.where(end, 2 + low * (1 - m), middle)

    def relay_copy(c):
        return remote(
            send_buf.at[c, far - 1], relay_buf.at[c], l_send.at[c], l_recv.at[c],
            {"wide": z + low},
        )

    def relay_arrival(c):
        return remote(
            relay_buf.at[c], relay_buf.at[c], l_send.at[c], l_recv.at[c], {"wide": z - low}
        )

    def place(o):
        return pl.ds(pl.multiple_of(column(o) * block, block), block)

    def part(c, m):
        k = turn(m)
        mix(c, lax.rem(z + k, n))
        if relay and m == n - 2:
            @pl.when(jnp.logical_not(end))
            def _():
                relay_arrival(c).wait_recv()
                for j in range(per_chunk):
                    send_buf[c, k - 1, j] = (added(c, j) + relay_buf[c, j].astype(F32)).astype(wire)

            @pl.when(end)
            def _():
                for j in range(per_chunk):
                    send_buf[c, k - 1, j] = added(c, j).astype(wire)
        else:
            for j in range(per_chunk):
                send_buf[c, k - 1, j] = added(c, j).astype(wire)
        if relay and m == 0:
            @pl.when(end)
            def _():
                relay_copy(c).start()

            @pl.when(jnp.logical_not(end))
            def _():
                sum_copy(c, k).start()
        else:
            sum_copy(c, k).start()

    for c in range(chunks):
        gather_finish(c)
        if c + 1 < chunks:
            for m in range(n - 1):
                part(c, m)
                gather_step(c + 1, m + 1)
        elif relay:
            for m in range(n - 1):
                part(c, m)
        else:
            pl.loop(0, n - 1)(functools.partial(part, c))
        mix(c, z)
        for j in range(per_chunk):
            out[:, place(c * per_chunk + j)] = added(c, j)

    def add_in(c, k):
        sum_copy(c, k).wait_recv()
        for j in range(per_chunk):
            out[:, place(c * per_chunk + j)] += recv_buf[c, k - 1, j].astype(F32)

    for c in range(chunks):
        if relay:
            for k in (2 - low, 2 + low):
                @pl.when((k == 2 + low) | jnp.logical_not(end))
                def _():
                    add_in(c, k)
            add_in(c, jnp.int32(2))
            for k in (2 - low, jnp.int32(2)):
                sum_copy(c, k).wait_send()

            @pl.when(end)
            def _():
                relay_copy(c).wait_send()

            @pl.when(jnp.logical_not(end))
            def _():
                sum_copy(c, far).wait_send()
        else:
            @pl.loop(0, n - 1)
            def _(m):
                k = turn(m)
                add_in(c, k)
                sum_copy(c, k).wait_send()

    for c in range(chunks):
        each_edge(c, 0, z, lambda *a: edge_copy(*a).wait_send())
        for stream in range(2):
            for step in range(1, n):
                @pl.when(z_sends(stream, step))
                def _():
                    z_copy(c, stream, step).wait_send()

                @pl.when(z_gets(stream, step))
                def _():
                    core_copy(c, stream, step, p).wait_send()
                    each_edge(
                        c, slot_of(stream, step), panel_of(stream, step),
                        lambda *a: edge_copy(*a).wait_send(),
                    )
    for copy in op_copies:
        copy.wait_send()


def local(n, nx, psi, left_ops, right_ops, left_source, right_shift, eps_left, eps_right):
    block = left_ops.shape[2]
    owned_terms, sectors = left_ops.shape[:2]
    out_rows = eps_left.shape[0]
    width = psi.shape[1]
    blocks = right_ops.shape[1]
    total = sectors * block
    terms = 2 * owned_terms
    group = math.gcd(out_rows, block)
    wire = jnp.bfloat16
    left = left_ops.reshape(owned_terms, n, 2, out_rows, block)
    shift = right_shift.reshape(1, owned_terms)
    slots = 2 * n - 1
    chunks = 2 if blocks % 2 == 0 and blocks >= 4 else 1
    per_chunk = blocks // chunks
    dma = pltpu.SemaphoreType.DMA
    hops = pl.pallas_call(
        functools.partial(kernel, n, nx, block, chunks, wire),
        out_shape=jax.ShapeDtypeStruct((out_rows, width), F32),
        in_specs=[pl.BlockSpec(memory_space=pl.ANY)] * 5
        + [pl.BlockSpec(memory_space=pltpu.SMEM)] * 2,
        out_specs=pl.BlockSpec(memory_space=pltpu.VMEM),
        scratch_shapes=[
            *[
                pltpu.VMEM((per_chunk + 2, total // group, group, block), jnp.bfloat16)
                for _ in range(chunks)
            ],
            pltpu.VMEM((terms, n, out_rows, block), jnp.bfloat16),
            pltpu.VMEM((blocks, block, terms * block), jnp.bfloat16),
            pltpu.VMEM((per_chunk, out_rows, terms * block), jnp.bfloat16),
            pltpu.VMEM((chunks, n - 1, per_chunk, out_rows, block), wire),
            pltpu.VMEM((chunks, n - 1, per_chunk, out_rows, block), wire),
            pltpu.VMEM((chunks, per_chunk, out_rows, block), wire),
            pltpu.VMEM(left_source.shape, jnp.int32),
            pltpu.SMEM(left_source.shape, jnp.int32),
            pltpu.VMEM(shift.shape, jnp.int32),
            pltpu.SMEM(shift.shape, jnp.int32),
            dma((blocks,)),
            dma((1 + owned_terms,)),
            dma((3 + owned_terms,)),
            dma((3 + owned_terms,)),
            dma((chunks, 2, n - 1)),
            dma((chunks, 2, n - 1)),
            dma((chunks, 2, n - 1)),
            dma((chunks, 2, n - 1)),
            dma((2, slots, 2)),
            dma((2, slots, 2)),
            dma((chunks, n - 1)),
            dma((chunks, n - 1)),
            dma((chunks,)),
            dma((chunks,)),
            dma((2,)),
            dma((2,)),
        ],
        compiler_params=pltpu.CompilerParams(
            collective_id=0, has_side_effects=True, vmem_limit_bytes=48 * 1024 * 1024
        ),
        cost_estimate=pl.CostEstimate(
            flops=4 * terms * n * out_rows * block * width,
            bytes_accessed=2 * (psi.size + left_ops.size + right_ops.size),
            transcendentals=0,
        ),
    )(psi.reshape(-1, group, width), left, right_ops, left_source, shift, left_source, shift)
    own = lax.dynamic_slice_in_dim(psi, lax.axis_index("pair") * out_rows, out_rows, 0).astype(F32)
    return hops + (eps_left[:, None] + eps_right[None, :]) * own


def solution(mesh):
    in_specs = (
        P(("groups", "wide"), "narrow"),
        P(("groups", "wide", "pair"), None, None, None),
        P(("groups", "wide", "pair"), "narrow", None, None),
        P(("wide", "pair"), None),
        P(("wide", "pair")),
        P(("groups", "wide", "pair")),
        P(("groups", "narrow")),
    )
    out_specs = P(("groups", "wide", "pair"), "narrow")
    body = functools.partial(local, mesh.shape["wide"], mesh.shape["narrow"])
    return jax.shard_map(body, mesh=mesh, in_specs=in_specs, out_specs=out_specs, check_vma=False)
```
